32 devices in a mesh: seq: 16 (over z, x, core), head: 2 (over y).
Axes of the slice: x: 2, y: 2, z: 4, core: 2. Of those that a mesh axis runs over, the one named last changes fastest.
Arguments:
- queries: bfloat16 [32768, 2048], P(('seq', 'head'))
- span_keys: bfloat16 [32768, 1024], P(('seq', 'head'))
- span_values: bfloat16 [32768, 1024], P(('seq', 'head')), may hold values from -6 to 6
- head_gates: bfloat16 [32768, 16], P(('seq', 'head')), may hold values from -8 to 8
- query_gain: float32 [128], replicated, may hold values from 0.5 to 5
- key_gain: float32 [128], replicated, may hold values from 0.5 to 5
- prompt_keys: bfloat16 [2, 1024, 8, 128], P(None, 'seq', 'head'), may hold values from -6 to 6
- prompt_values: bfloat16 [2, 1024, 8, 128], P(None, 'seq', 'head'), may hold values from -6 to 6
- prompt_length: int32 [2], replicated, may hold values from 1 to 1024, as said below
- request_group: int32 [16], replicated, may hold values from 0 to 1, as said below
Outputs:
- attended: bfloat16 [32768, 2048], P(('seq', 'head'))
- cache_keys: bfloat16 [16, 3072, 8, 128], P('seq', None, 'head')
- cache_values: bfloat16 [16, 3072, 8, 128], P('seq', None, 'head')
The draws below stay inside these ranges and needn't reach their ends.
Inputs may be any that keep to these rules, and one draw needn't show every extreme that they name: `prompt_length`: the largest length equals 1024 for some prompt. `request_group`: every prompt is used by at least one request.
All inputs are finite; a program needn't handle non-finite values.
Results may differ from the reference program's by a relative error of at most 0.0033.
The reference program's roundings to bfloat16 on the way (of `weights`) count: a program that leaves them out, or rounds other values in their place, can miss the bound.
Values may be sent and summed in bfloat16 or wider, within the bound.
A program may use at most 128 MiB of HBM per device.

```python
import math
import jax
import jax.numpy as jnp
from jax import lax

QH = 16
KVH = 8
HD = 128
SPAN = 2048
CACHE = 1024
REQUESTS = 16
GROUPS = 2
TOKENS = 32768


def shared_draw(key):
    query_draw = jax.random.normal(jax.random.fold_in(key, 11), (TOKENS, QH * HD), jnp.float32)
    key_draw = jax.random.normal(jax.random.fold_in(key, 12), (TOKENS, KVH * HD), jnp.float32)
    return (query_draw, key_draw)


def draw_queries(key, part):
    return shared_draw(key)[0].astype(jnp.bfloat16)


def draw_span_keys(key, part):
    return shared_draw(key)[1].astype(jnp.bfloat16)


def gain_draw(key):
    return jax.random.uniform(key, (HD,), jnp.float32, 0.5, 2.0)


def draw_query_gain(key, part):
    return gain_draw(jax.random.fold_in(key, 31))


def draw_key_gain(key, part):
    return gain_draw(jax.random.fold_in(key, 32))


def draw_prompt_length(key, part):
    lengths = jax.random.randint(jax.random.fold_in(key, 21), (GROUPS,), 1, CACHE + 1)
    longest = jax.random.randint(jax.random.fold_in(key, 22), (), 0, GROUPS)
    return lengths.at[longest].set(CACHE).astype(jnp.int32)


def draw_request_group(key, part):
    groups = jax.random.randint(jax.random.fold_in(key, 41), (REQUESTS,), 0, GROUPS)
    order = jax.random.permutation(jax.random.fold_in(key, 42), REQUESTS)
    groups = groups.at[order[:GROUPS]].set(jnp.arange(GROUPS, dtype=jnp.int32))
    return groups.astype(jnp.int32)


def steps_of(key, shape, split, smallest, high):
    level, own = 1.0, jax.random.fold_in(key, 6)
    for dim, blocks in split:
        steps = jnp.exp(jax.random.uniform(jax.random.fold_in(own, dim), (blocks,), jnp.float32, smallest / len(split), high / len(split)))
        level = level * jnp.repeat(steps, shape[dim] // blocks).reshape([-1 if axis == dim else 1 for axis in range(len(shape))])
    return level


def noise(own_key, extent, scale, limit, cuts=(), kind=jnp.bfloat16):
    array = scale * jax.random.normal(own_key, extent, jnp.float32)
    if cuts:
        array = array * steps_of(own_key, extent, cuts, -0.22, 0.18)
    return jnp.clip(array, -limit, limit).astype(kind)


def setup_inputs(seed: int = 0) -> dict:
    arg_keys = jax.random.split(jax.random.key(seed), 11)
    queries = draw_queries(jax.random.fold_in(arg_keys[10], 71), 0)
    span_keys = draw_span_keys(jax.random.fold_in(arg_keys[10], 71), 0)
    span_values = noise(arg_keys[2], (TOKENS, KVH * HD), 1.0, 6.0, ((0, 32),))
    head_gates = noise(arg_keys[3], (TOKENS, QH), 2.0, 8.0, ((0, 32),))
    query_gain = draw_query_gain(jax.random.fold_in(arg_keys[10], 71), 0)
    key_gain = draw_key_gain(jax.random.fold_in(arg_keys[10], 71), 0)
    prompt_keys = noise(arg_keys[6], (GROUPS, CACHE, KVH, HD), 1.0, 6.0, ((1, 16), (2, 2)))
    prompt_values = noise(arg_keys[7], (GROUPS, CACHE, KVH, HD), 1.0, 6.0, ((1, 16), (2, 2)))
    prompt_length = draw_prompt_length(jax.random.fold_in(arg_keys[10], 71), 0)
    request_group = draw_request_group(jax.random.fold_in(arg_keys[10], 71), 0)
    return dict(queries=queries, span_keys=span_keys, span_values=span_values, head_gates=head_gates, query_gain=query_gain, key_gain=key_gain, prompt_keys=prompt_keys, prompt_values=prompt_values, prompt_length=prompt_length, request_group=request_group)


def norm_rope(values_in, gain_vec, positions):
    head_dim = values_in.shape[-1]
    half_dim = head_dim // 2
    upcast = values_in.astype(jnp.float32)
    mean_sq = lax.optimization_barrier(jnp.mean(upcast * upcast, axis=-1, keepdims=True)) + 1e-06
    normed = upcast * lax.rsqrt(mean_sq) * gain_vec
    inv_freq = jnp.exp(-(jnp.arange(half_dim, dtype=jnp.float32) * (2.0 / head_dim)) * math.log(1000000.0))
    angles = positions[:, None] * inv_freq[None, :]
    cosine = jnp.cos(angles)[:, None, :]
    sine_part = jnp.sin(angles)[:, None, :]
    first_half = normed[..., :half_dim]
    second_half = normed[..., half_dim:]
    rotated = jnp.concatenate([first_half * cosine - second_half * sine_part, second_half * cosine + first_half * sine_part], axis=-1)
    return rotated.astype(jnp.bfloat16)

def attend(rotated_q, keys_all, values_all, gate_logits, length, cache_len):
    rows_total, kv_count, per_kv, head_dim = rotated_q.shape
    key_count = keys_all.shape[0]
    block_rows = min(512, rows_total)
    blocks = rows_total // block_rows
    key_pos = jnp.arange(key_count, dtype=jnp.int32)
    scale = 1.0 / math.sqrt(head_dim)

    def one_block(position):
        head_index = position // blocks
        row_start = position % blocks * block_rows
        kv_index = head_index // per_kv
        sub_index = head_index % per_kv
        query_block = lax.dynamic_slice(rotated_q, (row_start, kv_index, sub_index, jnp.int32(0)), (block_rows, 1, 1, head_dim)).reshape(block_rows, head_dim)
        key_head = lax.dynamic_index_in_dim(keys_all, kv_index, 1, keepdims=False)
        value_head = lax.dynamic_index_in_dim(values_all, kv_index, 1, keepdims=False)
        gate_block = lax.dynamic_slice(gate_logits, (row_start, kv_index, sub_index), (block_rows, 1, 1)).reshape(block_rows, 1)
        scores = jnp.dot(query_block.astype(jnp.float32), key_head.astype(jnp.float32).T, precision=lax.Precision.HIGHEST) * scale
        row_ids = row_start + jnp.arange(block_rows, dtype=jnp.int32)
        allowed = jnp.where(key_pos[None, :] < cache_len, key_pos[None, :] < length, key_pos[None, :] - cache_len <= row_ids[:, None])
        scores = jnp.where(allowed, scores, -1e+30)
        top_score = lax.optimization_barrier(jnp.max(scores, axis=-1, keepdims=True))
        raised = jnp.exp(scores - top_score)
        weights = (raised / lax.optimization_barrier(jnp.sum(raised, axis=-1, keepdims=True))).astype(jnp.bfloat16)
        mixed_out = jnp.dot(weights.astype(jnp.float32), value_head.astype(jnp.float32), precision=lax.Precision.HIGHEST)
        return (mixed_out * jax.nn.sigmoid(gate_block.astype(jnp.float32))).astype(jnp.bfloat16)
    outputs = lax.map(one_block, jnp.arange(kv_count * per_kv * blocks, dtype=jnp.int32))
    outputs = outputs.reshape(kv_count, per_kv, blocks, block_rows, head_dim)
    return outputs.transpose(2, 3, 0, 1, 4).reshape(rows_total, kv_count, per_kv, head_dim)

def append_span(prefix, span_rows, length):
    cache_len = prefix.shape[0]
    slot_pos = jnp.arange(cache_len, dtype=jnp.int32)
    kept = jnp.where((slot_pos < length)[:, None, None], prefix, jnp.zeros_like(prefix))
    base = jnp.concatenate([kept, jnp.zeros_like(span_rows)], axis=0)
    return lax.dynamic_update_slice_in_dim(base, span_rows, length, 0)

def reference(queries, span_keys, span_values, head_gates, query_gain, key_gain, prompt_keys, prompt_values, prompt_length, request_group):
    per_kv = QH // KVH

    def per_request(request):
        group = lax.dynamic_index_in_dim(request_group, request, 0, keepdims=False)
        length = lax.dynamic_index_in_dim(prompt_length, group, 0, keepdims=False)
        first = request * SPAN
        query_rows = lax.dynamic_slice_in_dim(queries, first, SPAN, 0).reshape(SPAN, QH, HD)
        key_rows = lax.dynamic_slice_in_dim(span_keys, first, SPAN, 0).reshape(SPAN, KVH, HD)
        value_rows = lax.dynamic_slice_in_dim(span_values, first, SPAN, 0).reshape(SPAN, KVH, HD)
        gate_rows = lax.dynamic_slice_in_dim(head_gates, first, SPAN, 0).reshape(SPAN, KVH, per_kv)
        positions = (length + jnp.arange(SPAN, dtype=jnp.int32)).astype(jnp.float32)
        rotated_q = norm_rope(query_rows, query_gain, positions).reshape(SPAN, KVH, per_kv, HD)
        rotated_k = norm_rope(key_rows, key_gain, positions)
        prefix_k = lax.dynamic_index_in_dim(prompt_keys, group, 0, keepdims=False)
        prefix_v = lax.dynamic_index_in_dim(prompt_values, group, 0, keepdims=False)
        keys_all = jnp.concatenate([prefix_k, rotated_k], axis=0)
        values_all = jnp.concatenate([prefix_v, value_rows], axis=0)
        result = attend(rotated_q, keys_all, values_all, gate_rows, length, CACHE).reshape(SPAN, QH * HD)
        return (result, append_span(prefix_k, rotated_k, length), append_span(prefix_v, value_rows, length))
    result, new_keys, new_values = lax.map(per_request, jnp.arange(REQUESTS, dtype=jnp.int32))
    return (result.reshape(TOKENS, QH * HD), new_keys, new_values)
```

```python
import functools
import math

import jax
import jax.numpy as jnp
from jax import lax
from jax.experimental import pallas as pl
from jax.experimental.pallas import tpu as pltpu
from jax.sharding import PartitionSpec as P

QH = 16
KVH = 8
HD = 128
PER = QH // KVH
BQ = 256
LOG2E = 1.4426950408889634


def norm_rope(x, gain, cosine, sine):
    x = x.astype(jnp.float32)
    mean_sq = jnp.mean(x * x, axis=-1, keepdims=True) + 1e-06
    n = x * lax.rsqrt(mean_sq) * gain
    return (n * cosine + pltpu.roll(n, HD // 2, 1) * sine).astype(jnp.bfloat16)


def attend_kernel(
    first_head,
    length_ref,
    rows_ref,
    prompt_ref,
    gate_ref,
    qgain_ref,
    kgain_ref,
    cos_ref,
    sin_ref,
    out_ref,
    key_ref,
):
    span = rows_ref.shape[0]
    cache_len = prompt_ref.shape[1]
    length = length_ref[0]
    head0 = length_ref[1] + first_head
    bq = min(BQ, span)
    blocks = span // bq
    const = LOG2E / math.sqrt(HD)

    @pl.loop(0, blocks)
    def _(i):
        at = pl.ds(pl.multiple_of(i * bq, bq), bq)
        key_ref[at, :] = norm_rope(
            rows_ref[at, PER * HD : (PER + 1) * HD], kgain_ref[...], cos_ref[at, :], sin_ref[at, :]
        )

    bias = jnp.where(lax.broadcasted_iota(jnp.int32, (1, cache_len), 1) < length, 0.0, -1e30)
    tri = lax.broadcasted_iota(jnp.int32, (bq, bq), 1) <= lax.broadcasted_iota(
        jnp.int32, (bq, bq), 0
    )
    nt = (((1,), (1,)), ((), ()))

    def scores(i, sub):
        at = slice(i * bq, (i + 1) * bq)
        q = norm_rope(
            rows_ref[at, sub * HD : (sub + 1) * HD], qgain_ref[...], cos_ref[at, :], sin_ref[at, :]
        )
        parts = [
            lax.dot_general(q, prompt_ref[0], nt, preferred_element_type=jnp.float32) + bias
        ]
        if i > 0:
            parts.append(
                lax.dot_general(q, key_ref[: i * bq, :], nt, preferred_element_type=jnp.float32)
            )
        diag = lax.dot_general(q, key_ref[at, :], nt, preferred_element_type=jnp.float32)
        parts.append(jnp.where(tri, diag, -1e30))
        top = functools.reduce(
            jnp.maximum, [jnp.max(p, axis=-1, keepdims=True) for p in parts]
        )
        return parts, top

    def finish(i, sub, parts, top):
        at = slice(i * bq, (i + 1) * bq)
        raised = [jnp.exp2((p - top) * const) for p in parts]
        total = sum(jnp.sum(p, axis=-1, keepdims=True) for p in raised)
        inverse = 1.0 / total
        weights = [(p * inverse).astype(jnp.bfloat16) for p in raised]
        vcol = slice((PER + 1) * HD, (PER + 2) * HD)
        values = [prompt_ref[1]]
        if i > 0:
            values.append(rows_ref[: i * bq, vcol])
        values.append(rows_ref[at, vcol])
        mixed = sum(
            jnp.dot(w, v, preferred_element_type=jnp.float32) for w, v in zip(weights, values)
        )
        gates = gate_ref[at, :].astype(jnp.float32)
        lane = lax.broadcasted_iota(jnp.int32, gates.shape, 1)
        gate = jnp.sum(jnp.where(lane == head0 + sub, gates, 0.0), axis=-1, keepdims=True)
        out_ref[at, sub * HD : (sub + 1) * HD] = (mixed * jax.nn.sigmoid(gate)).astype(
            jnp.bfloat16
        )

    for i in range(blocks):
        work = [(i, sub) + scores(i, sub) for sub in range(PER)]
        for item in work:
            finish(*item)


def attend(first_head, scalars, rows, prompt, gates, qgain, kgain, cosine, sine):
    span = rows.shape[0]
    cache_len = prompt.shape[1]
    vmem = pl.BlockSpec(memory_space=pltpu.VMEM)
    pairs = PER * span * (cache_len + span // 2)
    return pl.pallas_call(
        functools.partial(attend_kernel, first_head),
        out_shape=(
            jax.ShapeDtypeStruct((span, PER * HD), jnp.bfloat16),
            jax.ShapeDtypeStruct((span, HD), jnp.bfloat16),
        ),
        in_specs=[pl.BlockSpec(memory_space=pltpu.SMEM)] + [vmem] * 7,
        out_specs=(vmem, vmem),
        compiler_params=pltpu.CompilerParams(vmem_limit_bytes=48 * 1024 * 1024),
        cost_estimate=pl.CostEstimate(
            flops=8 * pairs * HD, bytes_accessed=6 * span * HD * 4, transcendentals=pairs
        ),
    )(scalars, rows, prompt, gates, qgain, kgain, cosine, sine)


def append_span(prefix, span_rows, length):
    cache_len = prefix.shape[0]
    slot_pos = jnp.arange(cache_len, dtype=jnp.int32)
    kept = jnp.where((slot_pos < length)[:, None], prefix, jnp.zeros_like(prefix))
    base = jnp.concatenate([kept, jnp.zeros_like(span_rows)], axis=0)
    return lax.dynamic_update_slice_in_dim(base, span_rows, length, 0)


def on_device(
    queries,
    span_keys,
    span_values,
    head_gates,
    query_gain,
    key_gain,
    prompt_keys,
    prompt_values,
    prompt_length,
    request_group,
):
    n = lax.axis_size("head")
    rows = queries.shape[0]
    span = rows * n
    kvl = KVH // n
    groups, part, _, _ = prompt_keys.shape
    group = lax.dynamic_index_in_dim(request_group, lax.axis_index("seq"), 0, keepdims=False)
    length = lax.dynamic_index_in_dim(prompt_length, group, 0, keepdims=False)
    scalars = jnp.stack([length, lax.axis_index("head") * (kvl * PER)]).astype(jnp.int32)

    gates = lax.all_gather(head_gates, "head", axis=0, tiled=True)
    received, prompts = [], []
    for c in range(kvl):
        pieces = []
        for d in range(n):
            head = d * kvl + c
            pieces.append(
                jnp.concatenate(
                    [
                        queries[:, head * PER * HD : (head + 1) * PER * HD],
                        span_keys[:, head * HD : (head + 1) * HD],
                        span_values[:, head * HD : (head + 1) * HD],
                    ],
                    axis=1,
                )
            )
        packed = jnp.stack(pieces)
        received.append(
            lax.all_to_all(packed, "head", split_axis=0, concat_axis=0, tiled=True).reshape(
                span, (PER + 2) * HD
            )
        )
        mine = jnp.stack([prompt_keys[:, :, c, :], prompt_values[:, :, c, :]])
        every = lax.all_gather(mine, "seq", axis=2, tiled=True)
        prompts.append(lax.dynamic_index_in_dim(every, group, 1, keepdims=False))
    cache_len = prompts[0].shape[1]

    positions = (length + jnp.arange(span, dtype=jnp.int32)).astype(jnp.float32)
    inv_freq = jnp.exp(
        -(jnp.arange(HD // 2, dtype=jnp.float32) * (2.0 / HD)) * math.log(1000000.0)
    )
    angles = positions[:, None] * inv_freq[None, :]
    cos_half, sin_half = jnp.cos(angles), jnp.sin(angles)
    cosine = jnp.concatenate([cos_half, cos_half], axis=1)
    sine = jnp.concatenate([-sin_half, sin_half], axis=1)

    keys, back = [], []
    for c in range(kvl):
        out, key = attend(
            c * PER,
            scalars,
            received[c],
            prompts[c],
            gates,
            query_gain[None],
            key_gain[None],
            cosine,
            sine,
        )
        keys.append(key)
        back.append(
            lax.all_to_all(
                out.reshape(n, rows, PER * HD), "head", split_axis=0, concat_axis=0, tiled=True
            )
        )
    attended = jnp.concatenate([back[c][d] for d in range(n) for c in range(kvl)], axis=1)
    vcol = (PER + 1) * HD
    new_keys = append_span(
        jnp.concatenate([p[0] for p in prompts], axis=1), jnp.concatenate(keys, axis=1), length
    )
    new_values = append_span(
        jnp.concatenate([p[1] for p in prompts], axis=1),
        jnp.concatenate([r[:, vcol:] for r in received], axis=1),
        length,
    )
    shape = (1, cache_len + span, kvl, HD)
    return (attended, new_keys.reshape(shape), new_values.reshape(shape))


def solution(mesh):
    token = P(("seq", "head"), None)
    prompt = P(None, "seq", "head", None)
    cache = P("seq", None, "head", None)
    return jax.shard_map(
        on_device,
        mesh=mesh,
        in_specs=(token, token, token, token, P(), P(), prompt, prompt, P(), P()),
        out_specs=(token, cache, cache),
        check_vma=False,
    )
```

```python
import functools
import math

import jax
import jax.numpy as jnp
from jax import lax
from jax.experimental import pallas as pl
from jax.experimental.pallas import tpu as pltpu
from jax.sharding import PartitionSpec as P

QH = 16
KVH = 8
HD = 128
PER = QH // KVH
BQ = 256
LOG2E = 1.4426950408889634


def norm_rope(x, gain, cosine, sine):
    x = x.astype(jnp.float32)
    mean_sq = jnp.mean(x * x, axis=-1, keepdims=True) + 1e-06
    n = x * lax.rsqrt(mean_sq) * gain
    return (n * cosine + pltpu.roll(n, HD // 2, 1) * sine).astype(jnp.bfloat16)


def attend_kernel(
    length_ref,
    rows_ref,
    prompt_ref,
    gate_ref,
    qgain_ref,
    kgain_ref,
    cos_ref,
    sin_ref,
    out_ref,
    key_ref,
    token_ref,
):
    token_ref[0] = length_ref[2]
    span = rows_ref.shape[0]
    cache_len = prompt_ref.shape[1]
    length = length_ref[0]
    head0 = length_ref[1]
    bq = min(BQ, span)
    blocks = span // bq
    const = LOG2E / math.sqrt(HD)

    @pl.loop(0, blocks)
    def _(i):
        at = pl.ds(pl.multiple_of(i * bq, bq), bq)
        key_ref[at, :] = norm_rope(
            rows_ref[at, PER * HD : (PER + 1) * HD], kgain_ref[...], cos_ref[at, :], sin_ref[at, :]
        )

    bias = jnp.where(lax.broadcasted_iota(jnp.int32, (1, cache_len), 1) < length, 0.0, -1e30)
    tri = lax.broadcasted_iota(jnp.int32, (bq, bq), 1) <= lax.broadcasted_iota(
        jnp.int32, (bq, bq), 0
    )
    nt = (((1,), (1,)), ((), ()))

    def scores(i, sub):
        at = slice(i * bq, (i + 1) * bq)
        q = norm_rope(
            rows_ref[at, sub * HD : (sub + 1) * HD], qgain_ref[...], cos_ref[at, :], sin_ref[at, :]
        )
        parts = [
            lax.dot_general(q, prompt_ref[0], nt, preferred_element_type=jnp.float32) + bias
        ]
        if i > 0:
            parts.append(
                lax.dot_general(q, key_ref[: i * bq, :], nt, preferred_element_type=jnp.float32)
            )
        diag = lax.dot_general(q, key_ref[at, :], nt, preferred_element_type=jnp.float32)
        parts.append(jnp.where(tri, diag, -1e30))
        top = functools.reduce(
            jnp.maximum, [jnp.max(p, axis=-1, keepdims=True) for p in parts]
        )
        return parts, top

    def finish(i, sub, parts, top):
        at = slice(i * bq, (i + 1) * bq)
        raised = [jnp.exp2((p - top) * const) for p in parts]
        total = sum(jnp.sum(p, axis=-1, keepdims=True) for p in raised)
        inverse = 1.0 / total
        weights = [(p * inverse).astype(jnp.bfloat16) for p in raised]
        vcol = slice((PER + 1) * HD, (PER + 2) * HD)
        values = [prompt_ref[1]]
        if i > 0:
            values.append(rows_ref[: i * bq, vcol])
        values.append(rows_ref[at, vcol])
        mixed = sum(
            jnp.dot(w, v, preferred_element_type=jnp.float32) for w, v in zip(weights, values)
        )
        gates = gate_ref[at, :].astype(jnp.float32)
        lane = lax.broadcasted_iota(jnp.int32, gates.shape, 1)
        gate = jnp.sum(jnp.where(lane == head0 + sub, gates, 0.0), axis=-1, keepdims=True)
        out_ref[at, sub * HD : (sub + 1) * HD] = (mixed * jax.nn.sigmoid(gate)).astype(
            jnp.bfloat16
        )

    for i in range(blocks):
        work = [(i, sub) + scores(i, sub) for sub in range(PER)]
        for item in work:
            finish(*item)


def attend(scalars, rows, prompt, gates, qgain, kgain, cosine, sine):
    span = rows.shape[0]
    cache_len = prompt.shape[1]
    vmem = pl.BlockSpec(memory_space=pltpu.VMEM)
    pairs = PER * span * (cache_len + span // 2)
    return pl.pallas_call(
        attend_kernel,
        out_shape=(
            jax.ShapeDtypeStruct((span, PER * HD), jnp.bfloat16),
            jax.ShapeDtypeStruct((span, HD), jnp.bfloat16),
            jax.ShapeDtypeStruct((1,), jnp.int32),
        ),
        in_specs=[pl.BlockSpec(memory_space=pltpu.SMEM)] + [vmem] * 7,
        out_specs=(vmem, vmem, pl.BlockSpec(memory_space=pltpu.SMEM)),
        compiler_params=pltpu.CompilerParams(vmem_limit_bytes=48 * 1024 * 1024),
        cost_estimate=pl.CostEstimate(
            flops=8 * pairs * HD, bytes_accessed=6 * span * HD * 4, transcendentals=pairs
        ),
    )(scalars, rows, prompt, gates, qgain, kgain, cosine, sine)


def append_span(prefix, span_rows, length):
    cache_len = prefix.shape[0]
    slot_pos = jnp.arange(cache_len, dtype=jnp.int32)
    kept = jnp.where((slot_pos < length)[:, None, None], prefix, jnp.zeros_like(prefix))
    base = jnp.concatenate([kept, jnp.zeros_like(span_rows)], axis=0)
    return lax.dynamic_update_slice_in_dim(base, span_rows, length, 0)


def on_device(
    queries,
    span_keys,
    span_values,
    head_gates,
    query_gain,
    key_gain,
    prompt_keys,
    prompt_values,
    prompt_length,
    request_group,
):
    n = lax.axis_size("head")
    rows = queries.shape[0]
    span = rows * n
    kvl = KVH // n
    groups, part, _, _ = prompt_keys.shape
    group = lax.dynamic_index_in_dim(request_group, lax.axis_index("seq"), 0, keepdims=False)
    length = lax.dynamic_index_in_dim(prompt_length, group, 0, keepdims=False)
    gates = lax.all_to_all(
        head_gates.T.reshape(n, kvl * PER, rows), "head", split_axis=0, concat_axis=0, tiled=True
    )
    gates = gates.transpose(0, 2, 1).reshape(span, kvl * PER)

    step = max(1, kvl // 2)
    gathered = []
    for c in range(0, kvl, step):
        mine = jnp.stack(
            [
                jnp.stack([p[:, :, c + k, :] for k in range(step)])
                for p in (prompt_keys, prompt_values)
            ],
            axis=1,
        )
        gathered.append(lax.all_gather(mine, "seq", axis=3, tiled=True))
    cache_len = gathered[0].shape[3]

    def send(pieces):
        return lax.all_to_all(pieces, "head", split_axis=0, concat_axis=0, tiled=True)

    def pack(c):
        def part(d):
            head = d * kvl + c
            return [
                queries[:, head * PER * HD : (head + 1) * PER * HD],
                span_keys[:, head * HD : (head + 1) * HD],
                span_values[:, head * HD : (head + 1) * HD],
            ]

        return jnp.stack([jnp.concatenate(part(d), axis=1) for d in range(n)])

    positions = (length + jnp.arange(span, dtype=jnp.int32)).astype(jnp.float32)
    inv_freq = jnp.exp(
        -(jnp.arange(HD // 2, dtype=jnp.float32) * (2.0 / HD)) * math.log(1000000.0)
    )
    angles = positions[:, None] * inv_freq[None, :]
    cos_half, sin_half = jnp.cos(angles), jnp.sin(angles)
    cosine = jnp.concatenate([cos_half, cos_half], axis=1)
    sine = jnp.concatenate([-sin_half, sin_half], axis=1)

    zero = jnp.int32(0)
    width = (PER + 2) * HD
    received = [send(pack(c)).reshape(span, width) for c in range(min(2, kvl))]
    keys, back, prompts = [], [], []
    token = zero
    for c in range(kvl):
        if c % step == 0:
            chosen = group + token
        prompts.append(
            lax.dynamic_index_in_dim(gathered[c // step][c % step], chosen, 1, keepdims=False)
        )
        out, key, mark = attend(
            jnp.stack([length, jnp.int32(c * PER), zero]),
            received[c],
            prompts[c],
            gates,
            query_gain[None],
            key_gain[None],
            cosine,
            sine,
        )
        token = mark[0]
        keys.append(key)
        out = out.reshape(n, rows, PER * HD)
        if c + 2 < kvl:
            both = send(jnp.concatenate([pack(c + 2), out], axis=2))
            received.append(both.reshape(span, width + PER * HD))
            back.append(both[:, :, width:])
        else:
            back.append(send(out))
    attended = jnp.concatenate([back[c][d] for d in range(n) for c in range(kvl)], axis=1)
    vcol = (PER + 1) * HD
    new_keys = append_span(
        jnp.stack([p[0] for p in prompts], axis=1), jnp.stack(keys, axis=1), length
    )
    new_values = append_span(
        jnp.stack([p[1] for p in prompts], axis=1),
        jnp.stack([r[:, vcol:width] for r in received], axis=1),
        length,
    )
    return (attended, new_keys[None], new_values[None])


def solution(mesh):
    token = P(("seq", "head"), None)
    prompt = P(None, "seq", "head", None)
    cache = P("seq", None, "head", None)
    return jax.shard_map(
        on_device,
        mesh=mesh,
        in_specs=(token, token, token, token, P(), P(), prompt, prompt, P(), P()),
        out_specs=(token, cache, cache),
        check_vma=False,
    )
```
